128 devices in a mesh: chan: 32 (over x, z, core), rep: 4 (over y).
Axes of the slice: x: 4, y: 4, z: 4, core: 2. Of those that a mesh axis runs over, the one named last changes fastest.
Arguments:
- block_sizes: int32 [64], P('chan'), may hold values from 64 to 2048, as said below
- amplitudes: bfloat16 [64, 2048, 384], P('chan'), may hold values from -6 to 6
- ladder_coupling: bfloat16 [64, 2048, 2048], P('chan', 'rep'), may hold values from -0.125 to 0.125
- bare_coupling: bfloat16 [64, 2048, 384], P('chan', 'rep'), may hold values from -6 to 6
- particle_energy: float32 [64, 2048], P('chan', 'rep'), may hold values from 0.5 to 8
- hole_energy: float32 [64, 384], P('chan'), may hold values from -8 to -0.5
- cycle_coupling: bfloat16 [192, 2048, 2048], P('chan', None, 'rep'), may hold values from -0.125 to 0.125
- pandya_rows: int32 [192, 2048], P('chan', 'rep'), may hold values from 0 to 131071, as said below
- pandya_weight: float32 [192, 2048], P('chan', 'rep'), may hold values from -1 to 1
Outputs:
- updated: bfloat16 [64, 2048, 384], P('chan', 'rep')
The draws below stay inside these ranges and needn't reach their ends.
Inputs may be any that keep to these rules, and one draw needn't show every extreme that they name: `block_sizes`: some channel has exactly 2048 valid rows. `pandya_rows`: take the particle-hole rows held by one device: channels q with the same q // 6, rows r with the same r // (2048 // 4). Among them, the rows naming particle-particle channels c with one value of c // 2 number at most 192, and exactly 192 for some value in every such group; those that also name rows p with one value of p // (2048 // 4) number at most 48, and exactly 48 for some values in every such group.
All inputs are finite; a program needn't handle non-finite values.
Results may differ from the reference program's by a relative error of at most 0.0095.
Values may be sent and summed in bfloat16 or wider, within the bound.
A program may use at most 128 MiB of HBM per device.

```python
import math
import jax
import jax.numpy as jnp
from jax import lax

CPP_DEV = 2
CPH_DEV = 6
PB = 2048
HB = 384
RB = 2048
NPP = 64
NPH = 192
PB_MIN = 64
N_CHAN = 32
N_REP = 4


def channel_sizes(key):
    drawn = jax.random.randint(key, (NPP,), PB_MIN, PB + 1)
    chosen = jax.random.randint(jax.random.fold_in(key, 7), (), 0, NPP)
    return jnp.where(jnp.arange(NPP) == chosen, PB, drawn).astype(jnp.int32)


def draw_block_sizes(key, part):
    return channel_sizes(key)


def draw_pandya_rows(key, part):
    key = jax.random.fold_in(key, 2)
    groups = N_CHAN * N_REP
    row_count = CPH_DEV * RB // N_REP
    average = row_count // N_CHAN
    share = PB // N_REP
    perm_keys = jax.random.split(jax.random.fold_in(key, 11), groups)
    orders = jax.vmap(lambda subkey: jax.random.permutation(subkey, N_CHAN))(perm_keys)
    spread = jax.random.randint(jax.random.fold_in(key, 12), (groups, N_CHAN // 2), 0, average + 1)
    spread = spread.at[:, 0].set(average)
    paired = jnp.stack([average + spread, average - spread], axis=2).reshape(groups, N_CHAN)
    counts = jax.vmap(lambda empty, where_to, amount: empty.at[where_to].set(amount))(jnp.zeros((groups, N_CHAN), jnp.int32), orders, paired)
    bounds = jnp.cumsum(counts, axis=1)
    position = jnp.arange(row_count, dtype=jnp.int32)
    source = jnp.sum((position[None, :, None] >= bounds[:, None, :]).astype(jnp.int32), axis=2)
    shuffle_keys = jax.random.split(jax.random.fold_in(key, 13), groups)
    shuffles = jax.vmap(lambda subkey: jax.random.permutation(subkey, row_count))(shuffle_keys)
    source = jnp.take_along_axis(source, shuffles, axis=1)
    onehot = (source[:, :, None] == jnp.arange(N_CHAN, dtype=jnp.int32)[None, None, :]).astype(jnp.int32)
    rank = jnp.sum(jnp.cumsum(onehot, axis=1) * onehot, axis=2) - 1
    quarter = rank % N_REP
    slot_index = jax.random.randint(jax.random.fold_in(key, 14), (groups, row_count), 0, CPP_DEV)
    channel = source * CPP_DEV + slot_index
    inner = jax.random.randint(jax.random.fold_in(key, 15), (groups, row_count), 0, share)
    row_index = quarter * share + inner
    global_row = (channel * PB + row_index).astype(jnp.int32)
    global_row = global_row.reshape(N_CHAN, N_REP, CPH_DEV, RB // N_REP).transpose(0, 2, 1, 3)
    return global_row.reshape(NPH, RB)


def level_of(own_key, extent, shards, low, high):
    gain, own = 1.0, jax.random.fold_in(own_key, 6)
    for dim, shards_of in shards:
        heights = jnp.exp(jax.random.uniform(jax.random.fold_in(own, dim), (shards_of,), jnp.float32, low / len(shards), high / len(shards)))
        gain = gain * jnp.repeat(heights, extent[dim] // shards_of).reshape([-1 if axis == dim else 1 for axis in range(len(extent))])
    return gain


def centred(stream_key, dims, scale, limit, shards=(), held_as=jnp.bfloat16):
    entries = scale * jax.random.normal(stream_key, dims, jnp.float32)
    if shards:
        entries = entries * level_of(stream_key, dims, shards, -0.22, 0.18)
    return jnp.clip(entries, -limit, limit).astype(held_as)


def setup_inputs(seed: int = 0) -> dict:
    arg_keys = jax.random.split(jax.random.key(seed), 10)
    return {
        "block_sizes": draw_block_sizes(jax.random.fold_in(arg_keys[9], 71), 0),
        "amplitudes": centred(arg_keys[1], (NPP, PB, HB), 1.0, 6.0, ((0, 32),)),
        "ladder_coupling": centred(arg_keys[2], (NPP, PB, PB), PB ** -0.5, 0.125, ((0, 32), (1, 4))),
        "bare_coupling": centred(arg_keys[3], (NPP, PB, HB), 1.0, 6.0, ((0, 32), (1, 4))),
        "particle_energy": jnp.clip(jnp.exp(math.log(8.0) - 2.7725887 * jax.random.uniform(arg_keys[4], (NPP, PB), jnp.float32) ** level_of(arg_keys[4], (NPP, PB), ((0, 32), (1, 4)), -0.2, 0.2)), 0.5, 8.0),
        "hole_energy": jnp.clip(-8.0 + 7.5 * jax.random.uniform(arg_keys[5], (NPP, HB), jnp.float32) ** level_of(arg_keys[5], (NPP, HB), ((0, 32),), -0.2, 0.2), -8.0, -0.5),
        "cycle_coupling": centred(arg_keys[6], (NPH, RB, RB), RB ** -0.5, 0.125, ((0, 32), (2, 4))),
        "pandya_rows": draw_pandya_rows(jax.random.fold_in(arg_keys[9], 71), 0),
        "pandya_weight": jnp.clip(jax.random.uniform(arg_keys[8], (NPH, RB), jnp.float32, -1.0, 1.0) * level_of(arg_keys[8], (NPH, RB), ((0, 32), (1, 4)), -0.4, 0.0), -1.0, 1.0),
    }


def cycle_block(operands):
    coupling, recoupled = operands
    quarter = RB // N_REP
    summed = jnp.zeros((RB, HB), jnp.float32)
    for group in range(N_REP):
        product = jnp.dot(coupling[:, group * quarter:(group + 1) * quarter], recoupled[group * quarter:(group + 1) * quarter], preferred_element_type=jnp.float32).astype(jnp.bfloat16)
        summed = summed + lax.optimization_barrier(product).astype(jnp.float32)
    return summed


def ladder_block(operands):
    coupling, amp_block, usable = operands
    masked = jnp.where(usable[:, None], amp_block, jnp.zeros_like(amp_block))
    return jnp.dot(coupling, masked, preferred_element_type=jnp.float32)


def reference(block_sizes, amplitudes, ladder_coupling, bare_coupling, particle_energy, hole_energy, cycle_coupling, pandya_rows, pandya_weight):
    flat_amp = amplitudes.reshape(NPP * PB, HB)
    pulled = flat_amp[pandya_rows]
    recoupled = (pandya_weight[:, :, None] * pulled.astype(jnp.float32)).astype(jnp.bfloat16)
    cycle_ph = lax.map(cycle_block, (cycle_coupling, recoupled))
    cycle_back = (pandya_weight[:, :, None] * cycle_ph).astype(jnp.bfloat16)
    cycle_pp = jnp.zeros((NPP * PB, HB), jnp.float32).at[pandya_rows.reshape(-1)].add(cycle_back.reshape(-1, HB).astype(jnp.float32))
    cycle_pp = cycle_pp.reshape(NPP, PB, HB)
    row_ids = jnp.arange(PB, dtype=jnp.int32)
    valid = row_ids[None, :] < block_sizes[:, None]
    ladder = lax.map(ladder_block, (ladder_coupling, amplitudes, valid))
    numer = bare_coupling.astype(jnp.float32) + 0.5 * ladder + cycle_pp
    denom = particle_energy[:, :, None] - hole_energy[:, None, :]
    result = jnp.where(valid[:, :, None], numer / denom, jnp.zeros_like(numer))
    return result.astype(jnp.bfloat16)
```

```python
import functools

import jax
import jax.numpy as jnp
from jax import lax
from jax.experimental import pallas as pl
from jax.experimental.pallas import tpu as pltpu
from jax.sharding import PartitionSpec as P

MESH = pl.DeviceIdType.MESH
BF = jnp.bfloat16
F32 = jnp.float32
I32 = jnp.int32

CHUNKS = ((0, 128), (128, 256))
CAP = 48
NT = (((1,), (1,)), ((), ()))


def dot(a, b):
    return jnp.dot(a, b, preferred_element_type=F32)


def iota(shape, dim):
    return lax.broadcasted_iota(I32, shape, dim)


def one_hot(mask):
    return jnp.where(mask, 1.0, 0.0).astype(BF)


def prep_kernel(rows_ref, weight_ref, energy_ref, slot_ref, back_ref, req_ref, cols_ref):
    blocks, width = rows_ref.shape
    upper = one_hot(iota((width, width), 0) <= iota((width, width), 1))
    key_ids = iota((256, width), 0)
    carry = jnp.zeros((256, 1), F32)
    tables = jnp.zeros((1024, 128), F32)
    for q in range(blocks):
        g = rows_ref[q : q + 1, :]
        chan = g >> 12
        quarter = (g >> 9) & 3
        inner = ((g >> 11) & 1) * 512 + (g & 511) + 1
        number = q * width + iota((1, width), 1) + 1
        hit = jnp.where(key_ids == chan * 8 + quarter, 1.0, 0.0)
        count = dot(hit.astype(BF), upper) + carry
        place = (jnp.sum(hit * count, axis=0, keepdims=True) - 1.0).astype(I32)
        carry = carry + jnp.sum(hit, axis=1, keepdims=True)
        at = one_hot(iota((128, width), 0) == place)
        parts = (inner >> 5, inner & 31, number >> 6, number & 63)
        values = jnp.concatenate([(hit * p.astype(F32)).astype(BF) for p in parts], axis=0)
        tables = tables + lax.dot_general(values, at, NT, preferred_element_type=F32)
        slot_ref[q : q + 1, :] = chan * (4 * CAP) + quarter * CAP + place
    req_ref[...] = (tables[0:256] * 32.0 + tables[256:512] - 1.0).astype(I32)
    back_ref[...] = jnp.maximum(tables[512:768] * 64.0 + tables[768:1024] - 1.0, 0.0).astype(I32)
    lanes = [weight_ref[q : q + 1, b * 128 : (b + 1) * 128] for q in range(blocks) for b in range(4)]
    lanes += [energy_ref[c : c + 1, b * 128 : (b + 1) * 128] for c in range(2) for b in range(4)]
    lanes.append(jnp.zeros((128 - len(lanes), 128), F32))
    cols_ref[...] = jnp.concatenate(lanes, axis=0).T


def prepare(rows, weight, energy):
    vmem = pl.BlockSpec(memory_space=pltpu.VMEM)
    return pl.pallas_call(
        prep_kernel,
        out_shape=(
            jax.ShapeDtypeStruct(rows.shape, I32),
            jax.ShapeDtypeStruct((256, 128), I32),
            jax.ShapeDtypeStruct((256, 128), I32),
            jax.ShapeDtypeStruct((128, 128), F32),
        ),
        in_specs=[vmem] * 3,
        out_specs=(vmem,) * 4,
    )(rows, weight, energy)


def main_kernel(
    slot_ref, back_ref, sizes_ref, req_ref, cols_ref, hole_ref, spread_ref, owner_ref, ownert_ref,
    amp_hbm, ladder_hbm, bare_hbm, cycle_hbm, out_ref,
    amp, bare, cyc, asked, mine, theirs, ordered, col, hot, x, rq, rec, stage, acc,
    *rest,
):
    n = len(CHUNKS)
    fs, fr, part, two, raw, comb, rv = (rest[i * n : (i + 1) * n] for i in range(7))
    (in_sem, cyc_sem, req_ss, req_rs, tab_ss, tab_rs,
     fwd_ss, fwd_rs, rs_ss, rs_rs, ret_ss, ret_rs) = rest[7 * n :]

    me = lax.axis_index("chan")
    my = lax.axis_index("rep")
    mx, mz, mc = lax.div(me, 8), lax.rem(lax.div(me, 2), 4), lax.rem(me, 2)

    def chan_of(dx, dz, dc, sign=1):
        xx = lax.rem(mx + sign * dx + 4, 4)
        zz = lax.rem(mz + sign * dz + 4, 4)
        return (xx * 4 + zz) * 2 + lax.rem(mc + dc, 2)

    def plane_peer(t):
        s = lax.rem(t * 13, 32)
        return chan_of(lax.rem(lax.div(s, 2), 4), lax.div(s, 8), lax.rem(s, 2))

    def cube_peer(t, sign=1):
        s = lax.rem(t * 45, 128)
        chan = chan_of(lax.rem(lax.div(s, 2), 4), lax.rem(lax.div(s, 8), 4), lax.rem(s, 2), sign)
        return chan, lax.rem(my + sign * lax.div(s, 32) + 4, 4)

    def rep_peer(d):
        return lax.rem(my + d, 4)

    def remote(src, dst, ss, rs, chan=None, rep=None):
        device = {}
        if chan is not None:
            device["chan"] = chan
        if rep is not None:
            device["rep"] = rep
        return pltpu.make_async_remote_copy(src, dst, ss, rs, device_id=device, device_id_type=MESH)

    amp_cp = pltpu.make_async_copy(amp_hbm, amp, in_sem.at[0])
    bare_cp = pltpu.make_async_copy(bare_hbm, bare, in_sem.at[1])
    amp_cp.start()
    bare_cp.start()
    lad_cps = [
        pltpu.make_async_copy(
            ladder_hbm.at[c, :, pl.ds(k * 512, 512)], cyc.at[c, pl.ds(k * 512, 512)], in_sem.at[2 + 4 * c + k]
        )
        for c in range(2)
        for k in range(4)
    ]
    for cp in lad_cps:
        cp.start()

    def cyc_copy(i):
        return pltpu.make_async_copy(cycle_hbm.at[i % 6], cyc.at[(i + 2) % 3], cyc_sem.at[(i + 2) % 3])

    cyc_copy(0).start()

    barrier = pltpu.get_barrier_semaphore()

    @pl.loop(1, 128)
    def _(t):
        chan, rep = cube_peer(t)
        pl.semaphore_signal(barrier, inc=1, device_id={"chan": chan, "rep": rep}, device_id_type=MESH)

    pl.semaphore_wait(barrier, 127)

    @pl.loop(1, 32)
    def _(t):
        p = plane_peer(t)
        remote(req_ref.at[p], asked.at[me], req_ss, req_rs, chan=p).start()

    asked[me] = req_ref[me]
    req_all = remote(req_ref.at[pl.ds(0, 31)], asked.at[pl.ds(0, 31)], req_ss, req_rs, chan=plane_peer(1))
    req_all.wait_recv()

    for q in range(4):
        mine[q] = asked[:, q, :]
    tab_cps = []
    for d in range(1, 4):
        to = rep_peer(d)
        cp = remote(mine.at[to], theirs.at[my], tab_ss.at[d - 1], tab_rs.at[d - 1], rep=to)
        cp.start()
        tab_cps.append(cp)
    theirs[my] = mine[my]

    def table_parts(table):
        t = table + 1
        return (t >> 5).astype(F32).astype(BF), (t & 31).astype(F32).astype(BF)

    for q in range(4):
        hi, lo = table_parts(mine[q])
        for b in range(4):
            rows = pl.ds(b * 384, 384)
            spread = spread_ref[rows, :]
            found = lax.dot_general(spread, hi, NT, preferred_element_type=F32) * 32.0
            found = found + lax.dot_general(spread, lo, NT, preferred_element_type=F32)
            found = jnp.sum(found * owner_ref[rows, :], axis=1, keepdims=True) - 1.0
            col[q, rows, :] = jnp.broadcast_to(found, (384, 128)).astype(I32)

    amp_cp.wait()

    def gather(k):
        c0, w = CHUNKS[k]

        @pl.loop(0, 4)
        def _(g):
            for q in range(4):
                for u in range(8):
                    p = plane_peer(g * 8 + u)
                    want = col[q, pl.ds(pl.multiple_of(p * CAP, CAP), CAP), :]
                    for b in range(8):
                        lane = iota((CAP, 128), 1) + b * 128
                        hot[u * CAP : (u + 1) * CAP, b * 128 : (b + 1) * 128] = one_hot(want == lane)
                got = dot(hot[:, 0:512], amp[0, q * 512 : (q + 1) * 512, c0 : c0 + w])
                got = got + dot(hot[:, 512:1024], amp[1, q * 512 : (q + 1) * 512, c0 : c0 + w])
                got = got.astype(BF)
                for u in range(8):
                    p = plane_peer(g * 8 + u)
                    fs[k][p, q * CAP : (q + 1) * CAP, :] = got[u * CAP : (u + 1) * CAP]

            for u in range(8):
                p = plane_peer(g * 8 + u)
                if u == 0:

                    @pl.when(g > 0)
                    def _():
                        remote(fs[k].at[p], fr[k].at[me], fwd_ss.at[k], fwd_rs.at[k], chan=p).start()
                else:
                    remote(fs[k].at[p], fr[k].at[me], fwd_ss.at[k], fwd_rs.at[k], chan=p).start()

        fr[k][me] = fs[k][me]

    for k in range(n):
        gather(k)

    bare_cp.wait()
    for c in range(2):
        for k in range(4):
            lad_cps[4 * c + k].wait()
        for k in range(4):
            usable = iota((512, 384), 0) + k * 512 < sizes_ref[c]
            block = amp[c, k * 512 : (k + 1) * 512, :].astype(F32)
            masked = jnp.where(usable, block, 0.0).astype(BF)
            term = 0.5 * dot(cyc[c, k * 512 : (k + 1) * 512, :], masked)
            if k == 0:
                acc[c * 512 : (c + 1) * 512, :] = bare[c].astype(F32) + term
            else:
                acc[c * 512 : (c + 1) * 512, :] += term
    cyc_copy(1).start()
    cyc_copy(2).start()

    for cp in tab_cps:
        cp.wait_recv()

    @pl.loop(0, 128)
    def _(t):
        chan, rep = cube_peer(t, -1)
        ordered[pl.ds(t, 1), :] = theirs[rep, pl.ds(chan, 1), :]

    def rs_copy(k, q, i):
        up, down = rep_peer(1), rep_peer(3)
        far = rep_peer(2) * 512
        rows = lambda start: part[k].at[q, pl.ds(pl.multiple_of(start, 256), 256)]
        args = (
            (rows(far), two[k].at[0, q], up),
            (rows(far + 256), two[k].at[1, q], down),
            (rows(up * 512 + 256), raw[k].at[0, q], up),
            (rows(down * 512), raw[k].at[1, q], down),
            (rows(up * 512), comb[k].at[0, q], up),
            (rows(down * 512 + 256), comb[k].at[1, q], down),
        )
        src, dst, to = args[i]
        return remote(src, dst, rs_ss.at[k, q, i], rs_rs.at[k, q, i], rep=to)

    def forward(k):
        c0, w = CHUNKS[k]
        done = remote(fs[k].at[pl.ds(0, 31)], fr[k].at[pl.ds(0, 31)], fwd_ss.at[k], fwd_rs.at[k], chan=plane_peer(1))
        done.wait_recv()
        done.wait_send()

        @pl.loop(0, 32)
        def _(s):
            for v in range(w // 128):
                x[v, pl.ds(pl.multiple_of(s * 192, 192), 192), :] = (
                    fr[k][s, :, v * 128 : (v + 1) * 128].astype(F32)
                )

        for q in range(6):

            @pl.loop(0, 32)
            def _(i):
                for u in range(16):
                    r = i * 16 + u
                    slot = slot_ref[q, r]
                    for v in range(w // 128):
                        rq[v, pl.ds(r, 1), :] = x[v, pl.ds(slot, 1), :]

            for b in range(4):
                rows = slice(b * 128, (b + 1) * 128)
                scale = jnp.broadcast_to(cols_ref[:, q * 4 + b : q * 4 + b + 1], (128, 128))
                for v in range(w // 128):
                    rec[rows, v * 128 : (v + 1) * 128] = (rq[v, rows, :] * scale).astype(BF)
            right = rec[:, 0:w]
            i = k * 6 + q
            cyc_copy(i).wait()
            for b in range(4):
                rows = slice(b * 512, (b + 1) * 512)
                part[k][q, rows, :] = dot(cyc[(i + 2) % 3, rows, :], right).astype(BF)
            if i + 3 < 6 * n:
                cyc_copy(i + 3).start()
            for j in range(4):
                rs_copy(k, q, j).start()
            if q >= 1:
                relay(k, q - 1)
        relay(k, 5)

    def relay(k, q):
        for j, start in ((0, rep_peer(1) * 512), (1, rep_peer(3) * 512 + 256)):
            rs_copy(k, q, j).wait_recv()
            rows = pl.ds(pl.multiple_of(start, 256), 256)
            part[k][q, rows, :] = (part[k][q, rows, :].astype(F32) + two[k][j, q].astype(F32)).astype(BF)
            rs_copy(k, q, 4 + j).start()

    def back(k):
        c0, w = CHUNKS[k]
        for q in range(6):
            for j in range(2, 6):
                rs_copy(k, q, j).wait_recv()
            for j in range(6):
                rs_copy(k, q, j).wait_send()
            for b in range(4):
                rows = pl.ds(pl.multiple_of(my * 512 + b * 128, 128), 128)
                half = slice((b % 2) * 128, (b % 2) * 128 + 128)
                if b < 2:
                    other = comb[k][0, q, half, :].astype(F32) + raw[k][1, q, half, :].astype(F32)
                else:
                    other = raw[k][0, q, half, :].astype(F32) + comb[k][1, q, half, :].astype(F32)
                total = part[k][q, rows, :].astype(F32) + other
                total = total * cols_ref[:, q * 4 + b : q * 4 + b + 1]
                for v in range(w // 128):
                    x[v, q * 512 + b * 128 : q * 512 + (b + 1) * 128, :] = total[:, v * 128 : (v + 1) * 128]

        def fill(t):
            chan, rep = cube_peer(t)
            key = chan * 8 + rep
            for j in range(CAP):
                row = back_ref[key, j]
                for v in range(w // 128):
                    stage[v, j : j + 1, :] = x[v, pl.ds(row, 1), :]
            rows = jnp.concatenate([stage[v] for v in range(w // 128)], axis=1)
            return chan, rep, rows.astype(BF)

        send = fs[k]
        chan, rep, rows = fill(0)
        rv[k][0] = rows

        @pl.loop(1, 128)
        def _(t):
            chan, rep, rows = fill(t)
            place = (lax.div(t, 4), pl.ds(pl.multiple_of(lax.rem(t, 4) * CAP, CAP), CAP))
            send[place[0], place[1], :] = rows
            remote(
                send.at[place[0], place[1]], rv[k].at[t], ret_ss.at[k], ret_rs.at[k, lax.div(t, 16)],
                chan=chan, rep=rep,
            ).start()

    def collect(k):
        c0, w = CHUNKS[k]
        for ph in range(8):
            first = 1 if ph == 0 else 0
            src = rv[k].at[pl.ds(ph * 16 + first, 16 - first)]
            chan, rep = cube_peer(1)
            remote(src, src, ret_ss.at[k], ret_rs.at[k, ph], chan=chan, rep=rep).wait_recv()
            hi, lo = table_parts(ordered[ph * 16 : (ph + 1) * 16, :])
            spread = spread_ref[0:768, :]
            found = lax.dot_general(hi, spread, NT, preferred_element_type=F32) * 32.0
            found = found + lax.dot_general(lo, spread, NT, preferred_element_type=F32)
            found = (jnp.sum(found * ownert_ref[...], axis=0, keepdims=True) - 1.0).astype(I32)
            rows = rv[k][ph * 16 : (ph + 1) * 16].reshape(16 * CAP, w)
            for b in range(4):
                at = one_hot(iota((256, 16 * CAP), 0) + b * 256 == found)
                acc[b * 256 : (b + 1) * 256, c0 : c0 + w] += dot(at, rows)
        for c in range(2):
            for b in range(4):
                rows = slice(c * 512 + b * 128, c * 512 + (b + 1) * 128)
                pe = cols_ref[:, 24 + c * 4 + b : 25 + c * 4 + b]
                value = acc[rows, c0 : c0 + w] / (pe - hole_ref[c : c + 1, c0 : c0 + w])
                usable = my * 512 + b * 128 + iota((128, w), 0) < sizes_ref[c]
                out_ref[c, b * 128 : (b + 1) * 128, c0 : c0 + w] = jnp.where(usable, value, 0.0).astype(BF)

    for k in range(n):
        forward(k)
        back(k)
    for k in range(n):
        collect(k)

    req_all.wait_send()
    for cp in tab_cps:
        cp.wait_send()
    chan, rep = cube_peer(1)
    for k in range(n):
        src = rv[k].at[pl.ds(0, 127)]
        remote(src, src, ret_ss.at[k], ret_rs.at[k, 0], chan=chan, rep=rep).wait_send()


def per_device(
    block_sizes, amplitudes, ladder_coupling, bare_coupling, particle_energy, hole_energy,
    cycle_coupling, pandya_rows, pandya_weight,
):
    slots, back, requests, cols = prepare(pandya_rows, pandya_weight, particle_energy)
    ids = jnp.arange(32 * CAP, dtype=I32)[:, None]
    lane = jnp.arange(128, dtype=I32)[None, :]
    spread = (ids % CAP == lane).astype(BF)
    owner = (ids // CAP == lane[:, :32]).astype(F32)
    ownert = (jnp.arange(16 * CAP, dtype=I32)[None, :] // CAP == jnp.arange(16, dtype=I32)[:, None]).astype(F32)
    vmem = pl.BlockSpec(memory_space=pltpu.VMEM)
    smem = pl.BlockSpec(memory_space=pltpu.SMEM)
    hbm = pl.BlockSpec(memory_space=pl.ANY)
    n = len(CHUNKS)
    ws = [w for _, w in CHUNKS]
    wide = max(ws)
    scratch = [
        pltpu.VMEM(amplitudes.shape, BF),
        pltpu.VMEM(bare_coupling.shape, BF),
        pltpu.VMEM((3, 2048, 512), BF),
        pltpu.VMEM((32, 8, 128), I32),
        pltpu.VMEM((4, 32, 128), I32),
        pltpu.VMEM((4, 32, 128), I32),
        pltpu.VMEM((128, 128), I32),
        pltpu.VMEM((4, 32 * CAP, 128), I32),
        pltpu.VMEM((8 * CAP, 1024), BF),
        pltpu.VMEM((wide // 128, 128 * CAP, 128), F32),
        pltpu.VMEM((wide // 128, 512, 128), F32),
        pltpu.VMEM((512, wide), BF),
        pltpu.VMEM((wide // 128, CAP, 128), F32),
        pltpu.VMEM((1024, 384), F32),
    ]
    scratch += [pltpu.VMEM((32, 4 * CAP, w), BF) for w in ws]
    scratch += [pltpu.VMEM((32, 4 * CAP, w), BF) for w in ws]
    scratch += [pltpu.VMEM((6, 2048, w), BF) for w in ws]
    for _ in range(3):
        scratch += [pltpu.VMEM((2, 6, 256, w), BF) for w in ws]
    scratch += [pltpu.VMEM((128, CAP, w), BF) for w in ws]
    sem = pltpu.SemaphoreType.DMA
    scratch += [
        sem((10,)), sem((3,)), sem, sem, sem((3,)), sem((3,)),
        sem((n,)), sem((n,)), sem((n, 6, 6)), sem((n, 6, 6)), sem((n,)), sem((n, 8)),
    ]
    return pl.pallas_call(
        main_kernel,
        out_shape=jax.ShapeDtypeStruct(bare_coupling.shape, BF),
        in_specs=[smem] * 3 + [vmem] * 6 + [hbm] * 4,
        out_specs=vmem,
        scratch_shapes=scratch,
        compiler_params=pltpu.CompilerParams(
            collective_id=0, has_side_effects=True, vmem_limit_bytes=60 * 1024 * 1024
        ),
        cost_estimate=pl.CostEstimate(flops=20_000_000_000, bytes_accessed=40_000_000, transcendentals=0),
    )(
        slots, back, block_sizes, requests.reshape(32, 8, 128), cols, hole_energy, spread, owner, ownert,
        amplitudes, ladder_coupling, bare_coupling, cycle_coupling,
    )


def solution(mesh):
    in_specs = (
        P("chan"),
        P("chan", None, None),
        P("chan", "rep", None),
        P("chan", "rep", None),
        P("chan", "rep"),
        P("chan", None),
        P("chan", None, "rep"),
        P("chan", "rep"),
        P("chan", "rep"),
    )
    out_specs = P("chan", "rep", None)
    return jax.shard_map(
        per_device, mesh=mesh, in_specs=in_specs, out_specs=out_specs, check_vma=False
    )
```

```python
import functools

import jax
import jax.numpy as jnp
from jax import lax
from jax.experimental import pallas as pl
from jax.experimental.pallas import tpu as pltpu
from jax.sharding import PartitionSpec as P

MESH = pl.DeviceIdType.MESH
BF = jnp.bfloat16
F32 = jnp.float32
I32 = jnp.int32

CHUNKS = 3
CAP = 48
LAG, TAIL = 2, 2
NT = (((1,), (1,)), ((), ()))


def dot(a, b):
    return jnp.dot(a, b, preferred_element_type=F32)


def iota(shape, dim):
    return lax.broadcasted_iota(I32, shape, dim)


def one_hot(mask):
    return jnp.where(mask, 1.0, 0.0).astype(BF)


def main_kernel(
    sizes_ref, rows_ref, weight_ref, energy_ref, hole_ref,
    amp_hbm, ladder_hbm, bare_hbm, cycle_hbm, out_ref,
    slot_ref, back_ref, slot_rows, back_rows, cols_ref, req_ref, amp, bare, cyc, asked, mine, spread, found_rows, col, hot, x, y, rq, rec, stage, acc,
    *rest,
):
    n = CHUNKS
    fs, fr, rv, part, two, raw, comb, fpart, ftwo, fraw, fcomb = (rest[i * n : (i + 1) * n] for i in range(11))
    (in_sem, cyc_sem, req_ss, req_rs, fwd_ss, fwd_rs, rs_ss, rs_rs, ret_ss, ret_rs, fin_ss, fin_rs) = rest[11 * n :]

    me = lax.axis_index("chan")
    my = lax.axis_index("rep")
    mx, mz, mc = lax.div(me, 8), lax.rem(lax.div(me, 2), 4), lax.rem(me, 2)
    up, down, far = lax.rem(my + 1, 4), lax.rem(my + 3, 4), lax.rem(my + 2, 4)

    def plane_peer(t):
        s = lax.rem(t * 13, 32)
        xx = lax.rem(mx + lax.rem(lax.div(s, 2), 4), 4)
        zz = lax.rem(mz + lax.div(s, 8), 4)
        return (xx * 4 + zz) * 2 + lax.rem(mc + lax.rem(s, 2), 2)

    def remote(src, dst, ss, rs, chan=None, rep=None):
        device = {"chan": chan} if rep is None else {"rep": rep}
        return pltpu.make_async_remote_copy(src, dst, ss, rs, device_id=device, device_id_type=MESH)

    def load(src, dst, i):
        cp = pltpu.make_async_copy(src, dst, in_sem.at[i])
        cp.start()
        return cp

    amp_cp = load(amp_hbm, amp, 0)
    bare_cp = load(bare_hbm, bare, 1)
    lad_cps = [
        load(ladder_hbm.at[c, :, pl.ds(k * 512, 512)], cyc.at[c, pl.ds(k * 512, 512)], 2 + 4 * c + k)
        for c in range(2)
        for k in range(4)
    ]

    def cyc_copy(i):
        return pltpu.make_async_copy(cycle_hbm.at[i % 6], cyc.at[(i + 2) % 3], cyc_sem.at[(i + 2) % 3])

    cyc_copy(0).start()

    barrier = pltpu.get_barrier_semaphore()

    @pl.loop(1, 32)
    def _(t):
        pl.semaphore_signal(barrier, inc=1, device_id={"chan": plane_peer(t)}, device_id_type=MESH)

    for to in (up, down):
        pl.semaphore_signal(barrier, inc=1, device_id={"rep": to}, device_id_type=MESH)

    blocks, width = rows_ref.shape
    key_ids = iota((128, width), 0)
    upper = one_hot(iota((width, width), 0) <= iota((width, width), 1))

    def keys(q):
        g = rows_ref[q : q + 1, :]
        return (g >> 12) * 4 + ((g >> 9) & 3), ((g >> 11) & 1) * 512 + (g & 511) + 1

    def by_slot(hit, place, value, bits):
        at = one_hot(key_ids == place)
        parts = (value >> bits, value & ((1 << bits) - 1))
        values = jnp.concatenate([(hit * p.astype(F32)).astype(BF) for p in parts], axis=0)
        return lax.dot_general(values, at, NT, preferred_element_type=F32)

    slot_rows[...] = jnp.zeros((8, width), I32)
    carry = jnp.zeros((128, 1), F32)
    table = jnp.zeros((256, 128), F32)
    for q in range(blocks):
        key, inner = keys(q)
        hit = jnp.where(key_ids == key, 1.0, 0.0)
        count = dot(hit.astype(BF), upper) + carry
        place = (jnp.sum(hit * count, axis=0, keepdims=True) - 1.0).astype(I32)
        carry = carry + jnp.sum(hit, axis=1, keepdims=True)
        table = table + by_slot(hit, place, inner, 5)
        slot_rows[q : q + 1, :] = jnp.clip(key * CAP + place, 0, 128 * CAP - 1)
    table = (table[0:128] * 32.0 + table[128:256] - 1.0).astype(I32)
    for c in range(32):
        req_ref[c] = table[c * 4 : c * 4 + 4]

    pl.semaphore_wait(barrier, 33)

    @pl.loop(1, 32)
    def _(t):
        p = plane_peer(t)
        remote(req_ref.at[p], asked.at[me], req_ss, req_rs, chan=p).start()

    asked[me] = req_ref[me]
    slots = iota((16 * CAP, 128), 0)
    lane = iota((16 * CAP, 128), 1)
    spread[...] = one_hot(slots - ((slots * 1366) >> 16) * CAP == lane)
    req_all = remote(req_ref.at[pl.ds(0, 31)], asked.at[pl.ds(0, 31)], req_ss, req_rs, chan=plane_peer(1))

    table = jnp.zeros((256, 128), F32)
    for q in range(blocks):
        key, _ = keys(q)
        hit = jnp.where(key_ids == key, 1.0, 0.0)
        number = q * width + iota((1, width), 1) + 1
        table = table + by_slot(hit, slot_rows[q : q + 1, :] - key * CAP, number, 6)
    back_rows[...] = jnp.clip((table[0:128] * 64.0 + table[128:256] - 1.0).astype(I32), 0, blocks * width - 1)
    slot_cp = load(slot_rows, slot_ref, 10)
    back_cp = load(back_rows, back_ref, 11)
    lanes = [weight_ref[q : q + 1, b * 128 : (b + 1) * 128] for q in range(blocks) for b in range(4)]
    lanes += [energy_ref[c : c + 1, b * 128 : (b + 1) * 128] for c in range(2) for b in range(4)]
    lanes.append(jnp.zeros((128 - len(lanes), 128), F32))
    cols_ref[...] = jnp.concatenate(lanes, axis=0).T
    req_all.wait_recv()

    for q in range(4):
        mine[q] = asked[:, q, :]

    def table_parts(table):
        t = table + 1
        return (t >> 5).astype(F32).astype(BF), (t & 31).astype(F32).astype(BF)

    def column(q):
        hi, lo = table_parts(mine[q])
        found = lax.dot_general(spread[0:384, :], hi, NT, preferred_element_type=F32) * 32.0
        found = found + lax.dot_general(spread[0:384, :], lo, NT, preferred_element_type=F32)
        owner = (iota((384, 32), 0) * 1366) >> 16
        for b in range(4):
            own = owner + b * 8 == iota((384, 32), 1)
            value = jnp.sum(jnp.where(own, found, 0.0), axis=1, keepdims=True) - 1.0
            col[q, b * 384 : (b + 1) * 384, :] = jnp.broadcast_to(value, (384, 128)).astype(I32)

    for q in range(4):
        column(q)
    amp_cp.wait()

    def gather(ks):
        c0, c1 = ks[0] * 128, ks[-1] * 128 + 128

        @pl.loop(0, 4)
        def _(g):
            for q in range(4):
                for u in range(8):
                    p = plane_peer(g * 8 + u)
                    want = col[q, pl.ds(pl.multiple_of(p * CAP, CAP), CAP), :]
                    for b in range(8):
                        at = iota((CAP, 128), 1) + b * 128
                        hot[u * CAP : (u + 1) * CAP, b * 128 : (b + 1) * 128] = one_hot(want == at)
                got = dot(hot[:, 0:512], amp[0, q * 512 : (q + 1) * 512, c0:c1])
                got = got + dot(hot[:, 512:1024], amp[1, q * 512 : (q + 1) * 512, c0:c1])
                got = got.astype(BF)
                for u in range(8):
                    p = plane_peer(g * 8 + u)
                    for j, k in enumerate(ks):
                        fs[k][p, q * CAP : (q + 1) * CAP, :] = got[u * CAP : (u + 1) * CAP, j * 128 : j * 128 + 128]

            for k in ks:
                for u in range(8):
                    p = plane_peer(g * 8 + u)

                    @pl.when(g * 8 + u > 0)
                    def _():
                        remote(fs[k].at[p], fr[k].at[me], fwd_ss.at[k], fwd_rs.at[k], chan=p).start()

        for k in ks:
            fr[k][me] = fs[k][me]

    gather((0,))
    gather((1, 2))

    bare_cp.wait()
    for c in range(2):
        for k in range(4):
            lad_cps[4 * c + k].wait()
        for k in range(4):
            usable = iota((512, 384), 0) + k * 512 < sizes_ref[c]
            block = amp[c, k * 512 : (k + 1) * 512, :].astype(F32)
            masked = jnp.where(usable, block, 0.0).astype(BF)
            term = 0.5 * dot(cyc[c, k * 512 : (k + 1) * 512, :], masked)
            if k == 0:
                acc[c * 512 : (c + 1) * 512, :] = bare[c].astype(F32) + term
            else:
                acc[c * 512 : (c + 1) * 512, :] += term
    cyc_copy(1).start()
    cyc_copy(2).start()

    quarters = (far, up, down, my)
    owner = (iota((16, 16 * CAP), 1) * 1366) >> 16
    for i, quarter in enumerate(quarters):
        for h in range(2):
            hi, lo = table_parts(mine[quarter, h * 16 : (h + 1) * 16, :])
            found = lax.dot_general(hi, spread[...], NT, preferred_element_type=F32) * 32.0
            found = found + lax.dot_general(lo, spread[...], NT, preferred_element_type=F32)
            found = jnp.where(owner == iota((16, 16 * CAP), 0), found, 0.0)
            value = jnp.sum(found, axis=0, keepdims=True) - 1.0
            found_rows[i : i + 1, h * 16 * CAP : (h + 1) * 16 * CAP] = value.astype(I32)

    def rs_copy(src, block, half, bufs, ss, rs, i):
        at = lambda where, h: src.at[pl.ds(pl.multiple_of(where * block + h * half, half), half)]
        b_two, b_raw, b_comb = bufs
        a, d, to = (
            (at(far, 0), b_two.at[0], up),
            (at(far, 1), b_two.at[1], down),
            (at(up, 1), b_raw.at[0], up),
            (at(down, 0), b_raw.at[1], down),
            (at(up, 0), b_comb.at[0], up),
            (at(down, 1), b_comb.at[1], down),
        )[i]
        return remote(a, d, ss.at[i], rs.at[i], rep=to)

    def cycle_rs(m, i):
        k, q = divmod(m, 6)
        bufs = (two[k].at[q], raw[k].at[q], comb[k].at[q])
        return rs_copy(part[k].at[q], 512, 256, bufs, rs_ss.at[k, q], rs_rs.at[k, q], i)

    def final_rs(k, i):
        return rs_copy(fpart[k], 1024, 512, (ftwo[k], fraw[k], fcomb[k]), fin_ss.at[k], fin_rs.at[k], i)

    def fwd_wait(k):
        done = remote(fs[k].at[pl.ds(0, 31)], fr[k].at[pl.ds(0, 31)], fwd_ss.at[k], fwd_rs.at[k], chan=plane_peer(1))
        done.wait_recv()
        done.wait_send()

        @pl.loop(0, 32)
        def _(s):
            x[pl.ds(pl.multiple_of(s * 192, 192), 192), :] = fr[k][s].astype(F32)

    def weight(q, b):
        return cols_ref[:, q * 4 + b : q * 4 + b + 1]

    def produce(m):
        k, q = divmod(m, 6)

        @pl.loop(0, 32)
        def _(i):
            for u in range(16):
                r = i * 16 + u
                rq[pl.ds(r, 1), :] = x[pl.ds(slot_ref[q, r], 1), :]

        for b in range(4):
            rows = slice(b * 128, (b + 1) * 128)
            rec[rows, :] = (rq[rows, :] * weight(q, b)).astype(BF)
        cyc_copy(m).wait()
        for b in range(4):
            rows = slice(b * 512, (b + 1) * 512)
            part[k][q, rows, :] = dot(cyc[(m + 2) % 3, rows, :], rec[...]).astype(BF)
        if m + 3 < 6 * n:
            cyc_copy(m + 3).start()
        for j in range(4):
            cycle_rs(m, j).start()

    def relay(m):
        k, q = divmod(m, 6)
        for j, start in ((0, up * 512), (1, down * 512 + 256)):
            cycle_rs(m, j).wait_recv()
            rows = pl.ds(pl.multiple_of(start, 256), 256)
            part[k][q, rows, :] = (part[k][q, rows, :].astype(F32) + two[k][q, j].astype(F32)).astype(BF)
            cycle_rs(m, 4 + j).start()

    def total(m):
        k, q = divmod(m, 6)
        for j in range(2, 6):
            cycle_rs(m, j).wait_recv()
        for b in range(4):
            rows = pl.ds(pl.multiple_of(my * 512 + b * 128, 128), 128)
            half = slice((b % 2) * 128, (b % 2) * 128 + 128)
            a, z = (comb[k], raw[k]) if b < 2 else (raw[k], comb[k])
            value = part[k][q, rows, :].astype(F32) + (a[q, 0, half, :].astype(F32) + z[q, 1, half, :].astype(F32))
            y[k % 2, q * 512 + b * 128 : q * 512 + (b + 1) * 128, :] = value * weight(q, b)

    def fill(k, p, q):
        for j in range(CAP):
            stage[j : j + 1, :] = y[k % 2, pl.ds(back_ref[p * 4 + q, j], 1), :]
        fs[k][p, pl.ds(pl.multiple_of(q * CAP, 16), CAP), :] = stage[...].astype(BF)

    def give_back(k, g):
        if g == 0:
            for q in range(4):
                fill(k, me, q)
            rv[k][me] = fs[k][me]

        @pl.loop(max(1, g * 8), g * 8 + 8)
        def _(t):
            p = plane_peer(t)
            for q in range(4):
                fill(k, p, q)
            remote(fs[k].at[p], rv[k].at[me], ret_ss.at[k], ret_rs.at[k, 0], chan=p).start()

    def quarter_copy(k, i, p):
        rows = pl.ds(pl.multiple_of(quarters[i] * CAP, 16), CAP)
        return remote(fs[k].at[p, rows], rv[k].at[me, rows], ret_ss.at[k], ret_rs.at[k, i], chan=p)

    def give_quarter(k, i):
        rows = pl.ds(pl.multiple_of(quarters[i] * CAP, 16), CAP)
        fill(k, me, quarters[i])
        rv[k][me, rows, :] = fs[k][me, rows, :]

        @pl.loop(1, 32)
        def _(t):
            p = plane_peer(t)
            fill(k, p, quarters[i])
            quarter_copy(k, i, p).start()

    def arrive(k, i):
        rows = pl.ds(0, 4 * CAP if k < n - 1 else CAP)
        src, dst = fs[k].at[pl.ds(0, 31), rows], rv[k].at[pl.ds(0, 31), rows]
        done = remote(src, dst, ret_ss.at[k], ret_rs.at[k, i], chan=plane_peer(1))
        done.wait_recv()
        done.wait_send()

    def collect(k, i):
        quarter = quarters[i]
        place = pl.ds(pl.multiple_of(quarter * CAP, 16), CAP)
        rows = rv[k][:, place, :].reshape(32 * CAP, 128)
        for b in range(4):
            at = one_hot(iota((256, 32 * CAP), 0) + b * 256 == found_rows[i : i + 1, :])
            value = dot(at, rows)
            if i < 3:
                where = pl.ds(pl.multiple_of(quarter * 1024 + b * 256, 256), 256)
                fpart[k][where, :] = value.astype(BF)
            else:
                acc[b * 256 : (b + 1) * 256, k * 128 : (k + 1) * 128] += value

    def send_on(k, i):
        for j in ((0, 1), (2,), (3,), ())[i]:
            final_rs(k, j).start()

    def final_relay(k):
        for j, start in ((0, up * 1024), (1, down * 1024 + 512)):
            final_rs(k, j).wait_recv()
            rows = pl.ds(pl.multiple_of(start, 512), 512)
            fpart[k][rows, :] = (fpart[k][rows, :].astype(F32) + ftwo[k][j].astype(F32)).astype(BF)
            final_rs(k, 4 + j).start()

    def finish(k):
        for j in range(2, 6):
            final_rs(k, j).wait_recv()
        cols = slice(k * 128, (k + 1) * 128)
        for c in range(2):
            a, z = ((fcomb[k], fraw[k]), (fraw[k], fcomb[k]))[c]
            for b in range(4):
                rows = slice(c * 512 + b * 128, c * 512 + (b + 1) * 128)
                half = slice(b * 128, (b + 1) * 128)
                other = a[0, half, :].astype(F32) + z[1, half, :].astype(F32)
                energy = cols_ref[:, 24 + c * 4 + b : 25 + c * 4 + b] - hole_ref[c : c + 1, cols]
                value = (acc[rows, cols] + other) / energy
                usable = my * 512 + b * 128 + iota((128, 128), 0) < sizes_ref[c]
                out_ref[c, half, cols] = jnp.where(usable, value, 0.0).astype(BF)

    slot_cp.wait()
    back_cp.wait()
    last = 6 * n
    for m in range(last + LAG + TAIL):
        if m < last:
            if m % 6 == 0:
                fwd_wait(m // 6)
            produce(m)
        if 0 <= m - LAG < last:
            relay(m - LAG)
            if m - LAG == last - 1:
                for i in range(4):
                    send_on(0, i)
        d = m - LAG - TAIL
        if 0 <= d < last:
            total(d)
            k, q = divmod(d, 6)
            if k > 0 and q < 2:
                give_back(k - 1, 2 * q)
                give_back(k - 1, 2 * q + 1)
            if d == 11:
                arrive(0, 0)
            if 11 <= d < 15:
                collect(0, d - 11)
    give_quarter(2, 0)
    give_quarter(2, 1)
    final_relay(0)
    give_quarter(2, 2)
    give_quarter(2, 3)
    arrive(1, 0)
    for i in range(4):
        collect(1, i)
        send_on(1, i)
    for i in range(4):
        arrive(2, i)
        collect(2, i)
        send_on(2, i)
        if i == 0:
            final_relay(1)
    finish(0)
    finish(1)
    final_relay(2)
    finish(2)

    req_all.wait_send()
    for m in range(last):
        for i in range(6):
            cycle_rs(m, i).wait_send()
    for k in range(n):
        for i in range(6):
            final_rs(k, i).wait_send()


def per_device(
    block_sizes, amplitudes, ladder_coupling, bare_coupling, particle_energy, hole_energy,
    cycle_coupling, pandya_rows, pandya_weight,
):
    vmem = pl.BlockSpec(memory_space=pltpu.VMEM)
    smem = pl.BlockSpec(memory_space=pltpu.SMEM)
    hbm = pl.BlockSpec(memory_space=pl.ANY)
    n = CHUNKS
    scratch = [
        pltpu.SMEM((8, 512), I32),
        pltpu.SMEM((128, 128), I32),
        pltpu.VMEM((8, 512), I32),
        pltpu.VMEM((128, 128), I32),
        pltpu.VMEM((128, 128), F32),
        pltpu.VMEM((32, 4, 128), I32),
        pltpu.VMEM(amplitudes.shape, BF),
        pltpu.VMEM(bare_coupling.shape, BF),
        pltpu.VMEM((3, 2048, 512), BF),
        pltpu.VMEM((32, 4, 128), I32),
        pltpu.VMEM((4, 32, 128), I32),
        pltpu.VMEM((16 * CAP, 128), BF),
        pltpu.VMEM((4, 32 * CAP), I32),
        pltpu.VMEM((4, 32 * CAP, 128), I32),
        pltpu.VMEM((8 * CAP, 1024), BF),
        pltpu.VMEM((128 * CAP, 128), F32),
        pltpu.VMEM((2, 3072, 128), F32),
        pltpu.VMEM((512, 128), F32),
        pltpu.VMEM((512, 128), BF),
        pltpu.VMEM((CAP, 128), F32),
        pltpu.VMEM((1024, 384), F32),
    ]
    for shape in (
        (32, 4 * CAP, 128), (32, 4 * CAP, 128), (32, 4 * CAP, 128), (6, 2048, 128),
        (6, 2, 256, 128), (6, 2, 256, 128), (6, 2, 256, 128),
        (4096, 128), (2, 512, 128), (2, 512, 128), (2, 512, 128),
    ):
        scratch += [pltpu.VMEM(shape, BF)] * n
    sem = pltpu.SemaphoreType.DMA
    scratch += [
        sem((12,)), sem((3,)), sem, sem, sem((n,)), sem((n,)), sem((n, 6, 6)), sem((n, 6, 6)),
        sem((n,)), sem((n, 4)), sem((n, 6)), sem((n, 6)),
    ]
    return pl.pallas_call(
        main_kernel,
        out_shape=jax.ShapeDtypeStruct(bare_coupling.shape, BF),
        in_specs=[smem] + [vmem] * 4 + [hbm] * 4,
        out_specs=vmem,
        scratch_shapes=scratch,
        compiler_params=pltpu.CompilerParams(
            collective_id=0, has_side_effects=True, vmem_limit_bytes=60 * 1024 * 1024
        ),
        cost_estimate=pl.CostEstimate(flops=20_000_000_000, bytes_accessed=40_000_000, transcendentals=0),
    )(
        block_sizes, pandya_rows, pandya_weight, particle_energy, hole_energy,
        amplitudes, ladder_coupling, bare_coupling, cycle_coupling,
    )


def solution(mesh):
    in_specs = (
        P("chan"),
        P("chan", None, None),
        P("chan", "rep", None),
        P("chan", "rep", None),
        P("chan", "rep"),
        P("chan", None),
        P("chan", None, "rep"),
        P("chan", "rep"),
        P("chan", "rep"),
    )
    out_specs = P("chan", "rep", None)
    return jax.shard_map(
        per_device, mesh=mesh, in_specs=in_specs, out_specs=out_specs, check_vma=False
    )
```

```python
import functools

import jax
import jax.numpy as jnp
from jax import lax
from jax.experimental import pallas as pl
from jax.experimental.pallas import tpu as pltpu
from jax.sharding import PartitionSpec as P

MESH = pl.DeviceIdType.MESH
BF = jnp.bfloat16
F32 = jnp.float32
I32 = jnp.int32

CHUNKS = 3
CAP = 48
LAG, TAIL = 2, 3
NT = (((1,), (1,)), ((), ()))


def dot(a, b):
    return jnp.dot(a, b, preferred_element_type=F32)


def iota(shape, dim):
    return lax.broadcasted_iota(I32, shape, dim)


def one_hot(mask):
    return jnp.where(mask, 1.0, 0.0).astype(BF)


def prep_kernel(rows_ref, weight_ref, energy_ref, slot_ref, back_ref, req_ref, cols_ref):
    blocks, width = rows_ref.shape
    key_ids = iota((128, width), 0)
    upper = one_hot(iota((width, width), 0) <= iota((width, width), 1))
    carry = jnp.zeros((128, 1), F32)
    tables = jnp.zeros((512, 128), F32)
    for q in range(blocks):
        g = rows_ref[q : q + 1, :]
        key = (g >> 12) * 4 + ((g >> 9) & 3)
        inner = ((g >> 11) & 1) * 512 + (g & 511) + 1
        number = q * width + iota((1, width), 1) + 1
        hit = jnp.where(key_ids == key, 1.0, 0.0)
        count = dot(hit.astype(BF), upper) + carry
        place = (jnp.sum(hit * count, axis=0, keepdims=True) - 1.0).astype(I32)
        carry = count[:, width - 1 : width]
        at = one_hot(key_ids == place)
        parts = (inner >> 5, inner & 31, number >> 6, number & 63)
        values = jnp.concatenate([(hit * p.astype(F32)).astype(BF) for p in parts], axis=0)
        tables = tables + lax.dot_general(values, at, NT, preferred_element_type=F32)
        slot_ref[q : q + 1, :] = key * CAP + place
    requests = (tables[0:128] * 32.0 + tables[128:256] - 1.0).astype(I32)
    for c in range(32):
        req_ref[c] = requests[c * 4 : c * 4 + 4]
    back_ref[...] = jnp.maximum(tables[256:384] * 64.0 + tables[384:512] - 1.0, 0.0).astype(I32)
    lanes = [weight_ref[q : q + 1, b * 128 : (b + 1) * 128] for q in range(blocks) for b in range(4)]
    lanes += [energy_ref[c : c + 1, b * 128 : (b + 1) * 128] for c in range(2) for b in range(4)]
    lanes.append(jnp.zeros((128 - len(lanes), 128), F32))
    cols_ref[...] = jnp.concatenate(lanes, axis=0).T


def prepare(rows, weight, energy):
    vmem = pl.BlockSpec(memory_space=pltpu.VMEM)
    return pl.pallas_call(
        prep_kernel,
        out_shape=(
            jax.ShapeDtypeStruct(rows.shape, I32),
            jax.ShapeDtypeStruct((128, 128), I32),
            jax.ShapeDtypeStruct((32, 4, 128), I32),
            jax.ShapeDtypeStruct((128, 128), F32),
        ),
        in_specs=[vmem] * 3,
        out_specs=(vmem,) * 4,
    )(rows, weight, energy)


def main_kernel(
    sizes_ref, slot_ref, back_ref, req_ref, cols_ref, hole_ref,
    amp_hbm, ladder_hbm, bare_hbm, cycle_hbm, out_ref,
    amp, bare, cyc, asked, mine, spread, found_rows, col, hot, x, y, rq, rec, stage, acc,
    *rest,
):
    n = CHUNKS
    fs, fr, rv, part, two, raw, comb, fpart, ftwo, fraw, fcomb = (rest[i * n : (i + 1) * n] for i in range(11))
    (in_sem, cyc_sem, req_ss, req_rs, fwd_ss, fwd_rs, rs_ss, rs_rs, ret_ss, ret_rs, fin_ss, fin_rs) = rest[11 * n :]

    me = lax.axis_index("chan")
    my = lax.axis_index("rep")
    mx, mz, mc = lax.div(me, 8), lax.rem(lax.div(me, 2), 4), lax.rem(me, 2)
    up, down, far = lax.rem(my + 1, 4), lax.rem(my + 3, 4), lax.rem(my + 2, 4)

    def plane_peer(t):
        s = lax.rem(t * 13, 32)
        xx = lax.rem(mx + lax.rem(lax.div(s, 2), 4), 4)
        zz = lax.rem(mz + lax.div(s, 8), 4)
        return (xx * 4 + zz) * 2 + lax.rem(mc + lax.rem(s, 2), 2)

    def remote(src, dst, ss, rs, chan=None, rep=None):
        device = {"chan": chan} if rep is None else {"rep": rep}
        return pltpu.make_async_remote_copy(src, dst, ss, rs, device_id=device, device_id_type=MESH)

    def load(src, dst, i):
        cp = pltpu.make_async_copy(src, dst, in_sem.at[i])
        cp.start()
        return cp

    amp_cp = load(amp_hbm, amp, 0)
    bare_cp = load(bare_hbm, bare, 1)
    lad_cps = [
        load(ladder_hbm.at[c, :, pl.ds(k * 512, 512)], cyc.at[c, pl.ds(k * 512, 512)], 2 + 4 * c + k)
        for c in range(2)
        for k in range(4)
    ]

    def cyc_copy(i):
        return pltpu.make_async_copy(cycle_hbm.at[i % 6], cyc.at[(i + 2) % 3], cyc_sem.at[(i + 2) % 3])

    cyc_copy(0).start()

    barrier = pltpu.get_barrier_semaphore()

    @pl.loop(1, 32)
    def _(t):
        pl.semaphore_signal(barrier, inc=1, device_id={"chan": plane_peer(t)}, device_id_type=MESH)

    for to in (up, down):
        pl.semaphore_signal(barrier, inc=1, device_id={"rep": to}, device_id_type=MESH)
    pl.semaphore_wait(barrier, 33)

    @pl.loop(1, 32)
    def _(t):
        p = plane_peer(t)
        remote(req_ref.at[p], asked.at[me], req_ss, req_rs, chan=p).start()

    asked[me] = req_ref[me]
    slots = iota((16 * CAP, 128), 0)
    lane = iota((16 * CAP, 128), 1)
    spread[...] = one_hot(slots - ((slots * 1366) >> 16) * CAP == lane)
    req_all = remote(req_ref.at[pl.ds(0, 31)], asked.at[pl.ds(0, 31)], req_ss, req_rs, chan=plane_peer(1))
    req_all.wait_recv()

    for q in range(4):
        mine[q] = asked[:, q, :]

    def table_parts(table):
        t = table + 1
        return (t >> 5).astype(F32).astype(BF), (t & 31).astype(F32).astype(BF)

    def column(q):
        hi, lo = table_parts(mine[q])
        found = lax.dot_general(spread[0:384, :], hi, NT, preferred_element_type=F32) * 32.0
        found = found + lax.dot_general(spread[0:384, :], lo, NT, preferred_element_type=F32)
        owner = (iota((384, 32), 0) * 1366) >> 16
        for b in range(4):
            own = owner + b * 8 == iota((384, 32), 1)
            value = jnp.sum(jnp.where(own, found, 0.0), axis=1, keepdims=True) - 1.0
            col[q, b * 384 : (b + 1) * 384, :] = jnp.broadcast_to(value, (384, 128)).astype(I32)

    for q in range(4):
        column(q)
    amp_cp.wait()

    def gather(ks):
        c0, c1 = ks[0] * 128, ks[-1] * 128 + 128

        @pl.loop(0, 4)
        def _(g):
            for q in range(4):
                for u in range(8):
                    p = plane_peer(g * 8 + u)
                    want = col[q, pl.ds(pl.multiple_of(p * CAP, CAP), CAP), :]
                    for b in range(8):
                        at = iota((CAP, 128), 1) + b * 128
                        hot[u * CAP : (u + 1) * CAP, b * 128 : (b + 1) * 128] = one_hot(want == at)
                got = dot(hot[:, 0:512], amp[0, q * 512 : (q + 1) * 512, c0:c1])
                got = got + dot(hot[:, 512:1024], amp[1, q * 512 : (q + 1) * 512, c0:c1])
                got = got.astype(BF)
                for u in range(8):
                    p = plane_peer(g * 8 + u)
                    for j, k in enumerate(ks):
                        fs[k][p, q * CAP : (q + 1) * CAP, :] = got[u * CAP : (u + 1) * CAP, j * 128 : j * 128 + 128]

            for k in ks:
                for u in range(8):
                    p = plane_peer(g * 8 + u)

                    @pl.when(g * 8 + u > 0)
                    def _():
                        remote(fs[k].at[p], fr[k].at[me], fwd_ss.at[k], fwd_rs.at[k], chan=p).start()

        for k in ks:
            fr[k][me] = fs[k][me]

    gather((0,))
    gather((1, 2))

    bare_cp.wait()
    for c in range(2):
        for k in range(4):
            lad_cps[4 * c + k].wait()
        for k in range(4):
            usable = iota((512, 384), 0) + k * 512 < sizes_ref[c]
            block = amp[c, k * 512 : (k + 1) * 512, :].astype(F32)
            masked = jnp.where(usable, block, 0.0).astype(BF)
            term = 0.5 * dot(cyc[c, k * 512 : (k + 1) * 512, :], masked)
            if k == 0:
                acc[c * 512 : (c + 1) * 512, :] = bare[c].astype(F32) + term
            else:
                acc[c * 512 : (c + 1) * 512, :] += term
    cyc_copy(1).start()
    cyc_copy(2).start()

    quarters = (far, up, down, my)
    owner = (iota((16, 16 * CAP), 1) * 1366) >> 16
    for i, quarter in enumerate(quarters):
        for h in range(2):
            hi, lo = table_parts(mine[quarter, h * 16 : (h + 1) * 16, :])
            found = lax.dot_general(hi, spread[...], NT, preferred_element_type=F32) * 32.0
            found = found + lax.dot_general(lo, spread[...], NT, preferred_element_type=F32)
            found = jnp.where(owner == iota((16, 16 * CAP), 0), found, 0.0)
            value = jnp.sum(found, axis=0, keepdims=True) - 1.0
            found_rows[i : i + 1, h * 16 * CAP : (h + 1) * 16 * CAP] = value.astype(I32)

    def rs_copy(src, block, half, bufs, ss, rs, i):
        at = lambda where, h: src.at[pl.ds(pl.multiple_of(where * block + h * half, half), half)]
        b_two, b_raw, b_comb = bufs
        a, d, to = (
            (at(far, 0), b_two.at[0], up),
            (at(far, 1), b_two.at[1], down),
            (at(up, 1), b_raw.at[0], up),
            (at(down, 0), b_raw.at[1], down),
            (at(up, 0), b_comb.at[0], up),
            (at(down, 1), b_comb.at[1], down),
        )[i]
        return remote(a, d, ss.at[i], rs.at[i], rep=to)

    def cycle_rs(m, i):
        k, q = divmod(m, 6)
        bufs = (two[k].at[q], raw[k].at[q], comb[k].at[q])
        return rs_copy(part[k].at[q], 512, 256, bufs, rs_ss.at[k, q], rs_rs.at[k, q], i)

    def final_rs(k, i):
        return rs_copy(fpart[k], 1024, 512, (ftwo[k], fraw[k], fcomb[k]), fin_ss.at[k], fin_rs.at[k], i)

    def fwd_wait(k):
        done = remote(fs[k].at[pl.ds(0, 31)], fr[k].at[pl.ds(0, 31)], fwd_ss.at[k], fwd_rs.at[k], chan=plane_peer(1))
        done.wait_recv()
        done.wait_send()

        @pl.loop(0, 32)
        def _(s):
            x[pl.ds(pl.multiple_of(s * 192, 192), 192), :] = fr[k][s].astype(F32)

    def weight(q, b):
        return cols_ref[:, q * 4 + b : q * 4 + b + 1]

    def produce(m):
        k, q = divmod(m, 6)

        @pl.loop(0, 32)
        def _(i):
            for u in range(16):
                r = i * 16 + u
                rq[pl.ds(r, 1), :] = x[pl.ds(slot_ref[q, r], 1), :]

        for b in range(4):
            rows = slice(b * 128, (b + 1) * 128)
            rec[rows, :] = (rq[rows, :] * weight(q, b)).astype(BF)
        cyc_copy(m).wait()
        for b in range(4):
            rows = slice(b * 512, (b + 1) * 512)
            part[k][q, rows, :] = dot(cyc[(m + 2) % 3, rows, :], rec[...]).astype(BF)
        if m + 3 < 6 * n:
            cyc_copy(m + 3).start()
        for j in range(4):
            cycle_rs(m, j).start()

    def relay(m):
        k, q = divmod(m, 6)
        for j, start in ((0, up * 512), (1, down * 512 + 256)):
            cycle_rs(m, j).wait_recv()
            rows = pl.ds(pl.multiple_of(start, 256), 256)
            part[k][q, rows, :] = (part[k][q, rows, :].astype(F32) + two[k][q, j].astype(F32)).astype(BF)
            cycle_rs(m, 4 + j).start()

    def total(m):
        k, q = divmod(m, 6)
        for j in range(2, 6):
            cycle_rs(m, j).wait_recv()
        for b in range(4):
            rows = pl.ds(pl.multiple_of(my * 512 + b * 128, 128), 128)
            half = slice((b % 2) * 128, (b % 2) * 128 + 128)
            a, z = (comb[k], raw[k]) if b < 2 else (raw[k], comb[k])
            value = part[k][q, rows, :].astype(F32) + (a[q, 0, half, :].astype(F32) + z[q, 1, half, :].astype(F32))
            y[k % 2, q * 512 + b * 128 : q * 512 + (b + 1) * 128, :] = value * weight(q, b)

    def fill(k, p, q):
        for j in range(CAP):
            stage[j : j + 1, :] = y[k % 2, pl.ds(back_ref[p * 4 + q, j], 1), :]
        fs[k][p, pl.ds(pl.multiple_of(q * CAP, 16), CAP), :] = stage[...].astype(BF)

    def give_back(k, g):
        if g == 0:
            for q in range(4):
                fill(k, me, q)
            rv[k][me] = fs[k][me]

        @pl.loop(max(1, g * 8), g * 8 + 8)
        def _(t):
            p = plane_peer(t)
            for q in range(4):
                fill(k, p, q)
            remote(fs[k].at[p], rv[k].at[me], ret_ss.at[k], ret_rs.at[k, 0], chan=p).start()

    def quarter_copy(k, i, p):
        rows = pl.ds(pl.multiple_of(quarters[i] * CAP, 16), CAP)
        return remote(fs[k].at[p, rows], rv[k].at[me, rows], ret_ss.at[k], ret_rs.at[k, i], chan=p)

    def give_quarter(k, i):
        rows = pl.ds(pl.multiple_of(quarters[i] * CAP, 16), CAP)
        fill(k, me, quarters[i])
        rv[k][me, rows, :] = fs[k][me, rows, :]

        @pl.loop(1, 32)
        def _(t):
            p = plane_peer(t)
            fill(k, p, quarters[i])
            quarter_copy(k, i, p).start()

    def arrive(k, i):
        rows = pl.ds(0, 4 * CAP if k < n - 1 else CAP)
        src, dst = fs[k].at[pl.ds(0, 31), rows], rv[k].at[pl.ds(0, 31), rows]
        done = remote(src, dst, ret_ss.at[k], ret_rs.at[k, i], chan=plane_peer(1))
        done.wait_recv()
        done.wait_send()

    def collect(k, i):
        quarter = quarters[i]
        place = pl.ds(pl.multiple_of(quarter * CAP, 16), CAP)
        rows = rv[k][:, place, :].reshape(32 * CAP, 128)
        for b in range(4):
            at = one_hot(iota((256, 32 * CAP), 0) + b * 256 == found_rows[i : i + 1, :])
            value = dot(at, rows)
            if i < 3:
                where = pl.ds(pl.multiple_of(quarter * 1024 + b * 256, 256), 256)
                fpart[k][where, :] = value.astype(BF)
            else:
                acc[b * 256 : (b + 1) * 256, k * 128 : (k + 1) * 128] += value

    def send_on(k, i):
        for j in ((0, 1), (2,), (3,), ())[i]:
            final_rs(k, j).start()

    def final_relay(k):
        for j, start in ((0, up * 1024), (1, down * 1024 + 512)):
            final_rs(k, j).wait_recv()
            rows = pl.ds(pl.multiple_of(start, 512), 512)
            fpart[k][rows, :] = (fpart[k][rows, :].astype(F32) + ftwo[k][j].astype(F32)).astype(BF)
            final_rs(k, 4 + j).start()

    def finish(k):
        for j in range(2, 6):
            final_rs(k, j).wait_recv()
        cols = slice(k * 128, (k + 1) * 128)
        for c in range(2):
            a, z = ((fcomb[k], fraw[k]), (fraw[k], fcomb[k]))[c]
            for b in range(4):
                rows = slice(c * 512 + b * 128, c * 512 + (b + 1) * 128)
                half = slice(b * 128, (b + 1) * 128)
                other = a[0, half, :].astype(F32) + z[1, half, :].astype(F32)
                energy = cols_ref[:, 24 + c * 4 + b : 25 + c * 4 + b] - hole_ref[c : c + 1, cols]
                value = (acc[rows, cols] + other) / energy
                usable = my * 512 + b * 128 + iota((128, 128), 0) < sizes_ref[c]
                out_ref[c, half, cols] = jnp.where(usable, value, 0.0).astype(BF)

    last = 6 * n
    for m in range(last + LAG + TAIL):
        if m < last:
            if m % 6 == 0:
                fwd_wait(m // 6)
            produce(m)
        if 0 <= m - LAG < last:
            relay(m - LAG)
        d = m - LAG - TAIL
        if 0 <= d < last:
            total(d)
            k, q = divmod(d, 6)
            if k > 0 and q < 4:
                give_back(k - 1, q)
            if d == 13:
                arrive(0, 0)
            if 13 <= d < 17:
                collect(0, d - 13)
    for i in range(4):
        send_on(0, i)
    for i in range(4):
        give_quarter(2, i)
    final_relay(0)
    arrive(1, 0)
    for i in range(4):
        collect(1, i)
        send_on(1, i)
    for i in range(4):
        arrive(2, i)
        collect(2, i)
        send_on(2, i)
        if i == 0:
            final_relay(1)
    finish(0)
    finish(1)
    final_relay(2)
    finish(2)

    req_all.wait_send()
    for m in range(last):
        for i in range(6):
            cycle_rs(m, i).wait_send()
    for k in range(n):
        for i in range(6):
            final_rs(k, i).wait_send()


def per_device(
    block_sizes, amplitudes, ladder_coupling, bare_coupling, particle_energy, hole_energy,
    cycle_coupling, pandya_rows, pandya_weight,
):
    slots, back, requests, cols = prepare(pandya_rows, pandya_weight, particle_energy)
    vmem = pl.BlockSpec(memory_space=pltpu.VMEM)
    smem = pl.BlockSpec(memory_space=pltpu.SMEM)
    hbm = pl.BlockSpec(memory_space=pl.ANY)
    n = CHUNKS
    scratch = [
        pltpu.VMEM(amplitudes.shape, BF),
        pltpu.VMEM(bare_coupling.shape, BF),
        pltpu.VMEM((3, 2048, 512), BF),
        pltpu.VMEM((32, 4, 128), I32),
        pltpu.VMEM((4, 32, 128), I32),
        pltpu.VMEM((16 * CAP, 128), BF),
        pltpu.VMEM((4, 32 * CAP), I32),
        pltpu.VMEM((4, 32 * CAP, 128), I32),
        pltpu.VMEM((8 * CAP, 1024), BF),
        pltpu.VMEM((128 * CAP, 128), F32),
        pltpu.VMEM((2, 3072, 128), F32),
        pltpu.VMEM((512, 128), F32),
        pltpu.VMEM((512, 128), BF),
        pltpu.VMEM((CAP, 128), F32),
        pltpu.VMEM((1024, 384), F32),
    ]
    for shape in (
        (32, 4 * CAP, 128), (32, 4 * CAP, 128), (32, 4 * CAP, 128), (6, 2048, 128),
        (6, 2, 256, 128), (6, 2, 256, 128), (6, 2, 256, 128),
        (4096, 128), (2, 512, 128), (2, 512, 128), (2, 512, 128),
    ):
        scratch += [pltpu.VMEM(shape, BF)] * n
    sem = pltpu.SemaphoreType.DMA
    scratch += [
        sem((10,)), sem((3,)), sem, sem, sem((n,)), sem((n,)), sem((n, 6, 6)), sem((n, 6, 6)),
        sem((n,)), sem((n, 4)), sem((n, 6)), sem((n, 6)),
    ]
    return pl.pallas_call(
        main_kernel,
        out_shape=jax.ShapeDtypeStruct(bare_coupling.shape, BF),
        in_specs=[smem] * 3 + [vmem] * 3 + [hbm] * 4,
        out_specs=vmem,
        scratch_shapes=scratch,
        compiler_params=pltpu.CompilerParams(
            collective_id=0, has_side_effects=True, vmem_limit_bytes=60 * 1024 * 1024
        ),
        cost_estimate=pl.CostEstimate(flops=20_000_000_000, bytes_accessed=40_000_000, transcendentals=0),
    )(
        block_sizes, slots, back, requests, cols, hole_energy,
        amplitudes, ladder_coupling, bare_coupling, cycle_coupling,
    )


def solution(mesh):
    in_specs = (
        P("chan"),
        P("chan", None, None),
        P("chan", "rep", None),
        P("chan", "rep", None),
        P("chan", "rep"),
        P("chan", None),
        P("chan", None, "rep"),
        P("chan", "rep"),
        P("chan", "rep"),
    )
    out_specs = P("chan", "rep", None)
    return jax.shard_map(
        per_device, mesh=mesh, in_specs=in_specs, out_specs=out_specs, check_vma=False
    )
```

```python
import functools

import jax
import jax.numpy as jnp
from jax import lax
from jax.experimental import pallas as pl
from jax.experimental.pallas import tpu as pltpu
from jax.sharding import PartitionSpec as P

MESH = pl.DeviceIdType.MESH
BF = jnp.bfloat16
F32 = jnp.float32
I32 = jnp.int32

CHUNKS = 3
CAP = 48
LAG, TAIL = 2, 2
NT = (((1,), (1,)), ((), ()))


def dot(a, b):
    return jnp.dot(a, b, preferred_element_type=F32)


def iota(shape, dim):
    return lax.broadcasted_iota(I32, shape, dim)


def one_hot(mask):
    return jnp.where(mask, 1.0, 0.0).astype(BF)


def main_kernel(
    sizes_ref, rows_ref, weight_ref, energy_ref, hole_ref,
    amp_hbm, ladder_hbm, bare_hbm, cycle_hbm, out_ref,
    slot_ref, back_ref, slot_rows, back_rows, cols_ref, req_ref, amp, bare, cyc, asked, mine, spread, found_rows, col, hot, x, y, rq, rec, stage, acc,
    *rest,
):
    n = CHUNKS
    fs, fr, rv, part, two, raw, comb, fpart, ftwo, fraw, fcomb = (rest[i * n : (i + 1) * n] for i in range(11))
    (in_sem, cyc_sem, req_ss, req_rs, fwd_ss, fwd_rs, rs_ss, rs_rs, ret_ss, ret_rs, fin_ss, fin_rs) = rest[11 * n :]

    me = lax.axis_index("chan")
    my = lax.axis_index("rep")
    mx, mz, mc = lax.div(me, 8), lax.rem(lax.div(me, 2), 4), lax.rem(me, 2)
    up, down, far = lax.rem(my + 1, 4), lax.rem(my + 3, 4), lax.rem(my + 2, 4)

    def plane_peer(t):
        s = lax.rem(t * 13, 32)
        xx = lax.rem(mx + lax.rem(lax.div(s, 2), 4), 4)
        zz = lax.rem(mz + lax.div(s, 8), 4)
        return (xx * 4 + zz) * 2 + lax.rem(mc + lax.rem(s, 2), 2)

    def remote(src, dst, ss, rs, chan=None, rep=None):
        device = {"chan": chan} if rep is None else {"rep": rep}
        return pltpu.make_async_remote_copy(src, dst, ss, rs, device_id=device, device_id_type=MESH)

    def load(src, dst, i):
        cp = pltpu.make_async_copy(src, dst, in_sem.at[i])
        cp.start()
        return cp

    amp_cp = load(amp_hbm, amp, 0)
    bare_cp = load(bare_hbm, bare, 1)
    lad_cps = [
        load(ladder_hbm.at[c, :, pl.ds(k * 512, 512)], cyc.at[c, pl.ds(k * 512, 512)], 2 + 4 * c + k)
        for c in range(2)
        for k in range(4)
    ]

    def cyc_copy(i):
        return pltpu.make_async_copy(cycle_hbm.at[i % 6], cyc.at[(i + 2) % 3], cyc_sem.at[(i + 2) % 3])

    cyc_copy(0).start()

    barrier = pltpu.get_barrier_semaphore()

    @pl.loop(1, 32)
    def _(t):
        pl.semaphore_signal(barrier, inc=1, device_id={"chan": plane_peer(t)}, device_id_type=MESH)

    for to in (up, down):
        pl.semaphore_signal(barrier, inc=1, device_id={"rep": to}, device_id_type=MESH)

    blocks, width = rows_ref.shape
    key_ids = iota((128, width), 0)
    upper = one_hot(iota((width, width), 0) <= iota((width, width), 1))

    def keys(q):
        g = rows_ref[q : q + 1, :]
        return (g >> 12) * 4 + ((g >> 9) & 3), ((g >> 11) & 1) * 512 + (g & 511) + 1

    def by_slot(hit, place, value, bits):
        at = one_hot(key_ids == place)
        parts = (value >> bits, value & ((1 << bits) - 1))
        values = jnp.concatenate([(hit * p.astype(F32)).astype(BF) for p in parts], axis=0)
        return lax.dot_general(values, at, NT, preferred_element_type=F32)

    slot_rows[...] = jnp.zeros((8, width), I32)
    carry = jnp.zeros((128, 1), F32)
    table = jnp.zeros((256, 128), F32)
    for q in range(blocks):
        key, inner = keys(q)
        hit = jnp.where(key_ids == key, 1.0, 0.0)
        count = dot(hit.astype(BF), upper) + carry
        place = (jnp.sum(hit * count, axis=0, keepdims=True) - 1.0).astype(I32)
        carry = carry + jnp.sum(hit, axis=1, keepdims=True)
        table = table + by_slot(hit, place, inner, 5)
        slot_rows[q : q + 1, :] = jnp.clip(key * CAP + place, 0, 128 * CAP - 1)
    table = (table[0:128] * 32.0 + table[128:256] - 1.0).astype(I32)
    for c in range(32):
        req_ref[c] = table[c * 4 : c * 4 + 4]

    pl.semaphore_wait(barrier, 33)

    @pl.loop(1, 32)
    def _(t):
        p = plane_peer(t)
        remote(req_ref.at[p], asked.at[me], req_ss, req_rs, chan=p).start()

    asked[me] = req_ref[me]
    slots = iota((16 * CAP, 128), 0)
    lane = iota((16 * CAP, 128), 1)
    spread[...] = one_hot(slots - ((slots * 1366) >> 16) * CAP == lane)
    req_all = remote(req_ref.at[pl.ds(0, 31)], asked.at[pl.ds(0, 31)], req_ss, req_rs, chan=plane_peer(1))

    table = jnp.zeros((256, 128), F32)
    for q in range(blocks):
        key, _ = keys(q)
        hit = jnp.where(key_ids == key, 1.0, 0.0)
        number = q * width + iota((1, width), 1) + 1
        table = table + by_slot(hit, slot_rows[q : q + 1, :] - key * CAP, number, 6)
    back_rows[...] = jnp.clip((table[0:128] * 64.0 + table[128:256] - 1.0).astype(I32), 0, blocks * width - 1)
    slot_cp = load(slot_rows, slot_ref, 10)
    back_cp = load(back_rows, back_ref, 11)
    lanes = [weight_ref[q : q + 1, b * 128 : (b + 1) * 128] for q in range(blocks) for b in range(4)]
    lanes += [energy_ref[c : c + 1, b * 128 : (b + 1) * 128] for c in range(2) for b in range(4)]
    lanes.append(jnp.zeros((128 - len(lanes), 128), F32))
    cols_ref[...] = jnp.concatenate(lanes, axis=0).T
    req_all.wait_recv()

    for q in range(4):
        mine[q] = asked[:, q, :]

    def table_parts(table):
        t = table + 1
        return (t >> 5).astype(F32).astype(BF), (t & 31).astype(F32).astype(BF)

    def column(q):
        hi, lo = table_parts(mine[q])
        found = lax.dot_general(spread[0:384, :], hi, NT, preferred_element_type=F32) * 32.0
        found = found + lax.dot_general(spread[0:384, :], lo, NT, preferred_element_type=F32)
        owner = (iota((384, 32), 0) * 1366) >> 16
        for b in range(4):
            own = owner + b * 8 == iota((384, 32), 1)
            value = jnp.sum(jnp.where(own, found, 0.0), axis=1, keepdims=True) - 1.0
            col[q, b * 384 : (b + 1) * 384, :] = jnp.broadcast_to(value, (384, 128)).astype(I32)

    for q in range(4):
        column(q)
    amp_cp.wait()

    def gather(ks):
        c0, c1 = ks[0] * 128, ks[-1] * 128 + 128

        @pl.loop(0, 4)
        def _(g):
            for q in range(4):
                for u in range(8):
                    p = plane_peer(g * 8 + u)
                    want = col[q, pl.ds(pl.multiple_of(p * CAP, CAP), CAP), :]
                    for b in range(8):
                        at = iota((CAP, 128), 1) + b * 128
                        hot[u * CAP : (u + 1) * CAP, b * 128 : (b + 1) * 128] = one_hot(want == at)
                got = dot(hot[:, 0:512], amp[0, q * 512 : (q + 1) * 512, c0:c1])
                got = got + dot(hot[:, 512:1024], amp[1, q * 512 : (q + 1) * 512, c0:c1])
                got = got.astype(BF)
                for u in range(8):
                    p = plane_peer(g * 8 + u)
                    for j, k in enumerate(ks):
                        fs[k][p, q * CAP : (q + 1) * CAP, :] = got[u * CAP : (u + 1) * CAP, j * 128 : j * 128 + 128]

            for k in ks:
                for u in range(8):
                    p = plane_peer(g * 8 + u)

                    @pl.when(g * 8 + u > 0)
                    def _():
                        remote(fs[k].at[p], fr[k].at[me], fwd_ss.at[k], fwd_rs.at[k], chan=p).start()

        for k in ks:
            fr[k][me] = fs[k][me]

    gather((0,))
    gather((1, 2))

    bare_cp.wait()
    for c in range(2):
        for k in range(4):
            lad_cps[4 * c + k].wait()
        acc[c * 512 : (c + 1) * 512, :] = bare[c].astype(F32)

        @pl.loop(0, 4)
        def _(k):
            rows = pl.ds(pl.multiple_of(k * 512, 512), 512)
            usable = iota((512, 384), 0) + k * 512 < sizes_ref[c]
            masked = jnp.where(usable, amp[c, rows, :].astype(F32), 0.0).astype(BF)
            acc[c * 512 : (c + 1) * 512, :] += 0.5 * dot(cyc[c, rows, :], masked)
    cyc_copy(1).start()
    cyc_copy(2).start()

    quarters = (far, up, down, my)
    owner = (iota((16, 16 * CAP), 1) * 1366) >> 16
    for i, quarter in enumerate(quarters):
        for h in range(2):
            hi, lo = table_parts(mine[quarter, h * 16 : (h + 1) * 16, :])
            found = lax.dot_general(hi, spread[...], NT, preferred_element_type=F32) * 32.0
            found = found + lax.dot_general(lo, spread[...], NT, preferred_element_type=F32)
            found = jnp.where(owner == iota((16, 16 * CAP), 0), found, 0.0)
            value = jnp.sum(found, axis=0, keepdims=True) - 1.0
            found_rows[i : i + 1, h * 16 * CAP : (h + 1) * 16 * CAP] = value.astype(I32)

    def rs_copy(src, block, half, bufs, ss, rs, i):
        at = lambda where, h: src.at[pl.ds(pl.multiple_of(where * block + h * half, half), half)]
        b_two, b_raw, b_comb = bufs
        a, d, to = (
            (at(far, 0), b_two.at[0], up),
            (at(far, 1), b_two.at[1], down),
            (at(up, 1), b_raw.at[0], up),
            (at(down, 0), b_raw.at[1], down),
            (at(up, 0), b_comb.at[0], up),
            (at(down, 1), b_comb.at[1], down),
        )[i]
        return remote(a, d, ss.at[i], rs.at[i], rep=to)

    def cycle_rs(m, i):
        k, q = divmod(m, 6)
        bufs = (two[k].at[q], raw[k].at[q], comb[k].at[q])
        return rs_copy(part[k].at[q], 512, 256, bufs, rs_ss.at[k, q], rs_rs.at[k, q], i)

    def final_rs(k, i):
        return rs_copy(fpart[k], 1024, 512, (ftwo[k], fraw[k], fcomb[k]), fin_ss.at[k], fin_rs.at[k], i)

    def fwd_wait(k):
        done = remote(fs[k].at[pl.ds(0, 31)], fr[k].at[pl.ds(0, 31)], fwd_ss.at[k], fwd_rs.at[k], chan=plane_peer(1))
        done.wait_recv()
        done.wait_send()

        @pl.loop(0, 32)
        def _(s):
            x[pl.ds(pl.multiple_of(s * 192, 192), 192), :] = fr[k][s].astype(F32)

    def weight(q, b):
        return cols_ref[:, q * 4 + b : q * 4 + b + 1]

    def produce(m):
        k, q = divmod(m, 6)

        @pl.loop(0, 32)
        def _(i):
            for u in range(16):
                r = i * 16 + u
                rq[pl.ds(r, 1), :] = x[pl.ds(slot_ref[q, r], 1), :]

        for b in range(4):
            rows = slice(b * 128, (b + 1) * 128)
            rec[rows, :] = (rq[rows, :] * weight(q, b)).astype(BF)
        cyc_copy(m).wait()

        @pl.loop(0, 4)
        def _(b):
            rows = pl.ds(pl.multiple_of(b * 512, 512), 512)
            part[k][q, rows, :] = dot(cyc[(m + 2) % 3, rows, :], rec[...]).astype(BF)
        if m + 3 < 6 * n:
            cyc_copy(m + 3).start()
        for j in range(4):
            cycle_rs(m, j).start()

    def relay(m):
        k, q = divmod(m, 6)
        for j, start in ((0, up * 512), (1, down * 512 + 256)):
            cycle_rs(m, j).wait_recv()
            rows = pl.ds(pl.multiple_of(start, 256), 256)
            part[k][q, rows, :] = (part[k][q, rows, :].astype(F32) + two[k][q, j].astype(F32)).astype(BF)
            cycle_rs(m, 4 + j).start()

    def total(m):
        k, q = divmod(m, 6)
        for j in range(2, 6):
            cycle_rs(m, j).wait_recv()
        for b in range(4):
            rows = pl.ds(pl.multiple_of(my * 512 + b * 128, 128), 128)
            half = slice((b % 2) * 128, (b % 2) * 128 + 128)
            a, z = (comb[k], raw[k]) if b < 2 else (raw[k], comb[k])
            value = part[k][q, rows, :].astype(F32) + (a[q, 0, half, :].astype(F32) + z[q, 1, half, :].astype(F32))
            y[k % 2, q * 512 + b * 128 : q * 512 + (b + 1) * 128, :] = value * weight(q, b)

    def fill(k, p, q):
        @pl.loop(0, 3)
        def _(b):
            for u in range(16):
                j = b * 16 + u
                stage[pl.ds(j, 1), :] = y[k % 2, pl.ds(back_ref[p * 4 + q, j], 1), :]

        fs[k][p, pl.ds(pl.multiple_of(q * CAP, 16), CAP), :] = stage[...].astype(BF)

    def give_back(k, g):
        if g == 0:
            pl.loop(0, 4)(lambda q: fill(k, me, q))
            rv[k][me] = fs[k][me]

        @pl.loop(max(1, g * 8), g * 8 + 8)
        def _(t):
            p = plane_peer(t)
            pl.loop(0, 4)(lambda q: fill(k, p, q))
            remote(fs[k].at[p], rv[k].at[me], ret_ss.at[k], ret_rs.at[k, 0], chan=p).start()

    def quarter_copy(k, i, p):
        rows = pl.ds(pl.multiple_of(quarters[i] * CAP, 16), CAP)
        return remote(fs[k].at[p, rows], rv[k].at[me, rows], ret_ss.at[k], ret_rs.at[k, i], chan=p)

    def give_quarter(k, i):
        rows = pl.ds(pl.multiple_of(quarters[i] * CAP, 16), CAP)
        fill(k, me, quarters[i])
        rv[k][me, rows, :] = fs[k][me, rows, :]

        @pl.loop(1, 32)
        def _(t):
            p = plane_peer(t)
            fill(k, p, quarters[i])
            quarter_copy(k, i, p).start()

    def arrive(k, i):
        rows = pl.ds(0, 4 * CAP if k < n - 1 else CAP)
        src, dst = fs[k].at[pl.ds(0, 31), rows], rv[k].at[pl.ds(0, 31), rows]
        done = remote(src, dst, ret_ss.at[k], ret_rs.at[k, i], chan=plane_peer(1))
        done.wait_recv()
        done.wait_send()

    def collect(k, i):
        quarter = quarters[i]
        place = pl.ds(pl.multiple_of(quarter * CAP, 16), CAP)
        rows = rv[k][:, place, :].reshape(32 * CAP, 128)

        @pl.loop(0, 4)
        def _(b):
            at = one_hot(iota((256, 32 * CAP), 0) + b * 256 == found_rows[i : i + 1, :])
            value = dot(at, rows)
            if i < 3:
                where = pl.ds(pl.multiple_of(quarter * 1024 + b * 256, 256), 256)
                fpart[k][where, :] = value.astype(BF)
            else:
                acc[pl.ds(pl.multiple_of(b * 256, 256), 256), k * 128 : (k + 1) * 128] += value

    def send_on(k, i):
        for j in ((0, 1), (2,), (3,), ())[i]:
            final_rs(k, j).start()

    def final_relay(k):
        for j, start in ((0, up * 1024), (1, down * 1024 + 512)):
            final_rs(k, j).wait_recv()
            rows = pl.ds(pl.multiple_of(start, 512), 512)
            fpart[k][rows, :] = (fpart[k][rows, :].astype(F32) + ftwo[k][j].astype(F32)).astype(BF)
            final_rs(k, 4 + j).start()

    def finish(k):
        for j in range(2, 6):
            final_rs(k, j).wait_recv()
        cols = slice(k * 128, (k + 1) * 128)
        for c in range(2):
            a, z = ((fcomb[k], fraw[k]), (fraw[k], fcomb[k]))[c]
            for b in range(4):
                rows = slice(c * 512 + b * 128, c * 512 + (b + 1) * 128)
                half = slice(b * 128, (b + 1) * 128)
                other = a[0, half, :].astype(F32) + z[1, half, :].astype(F32)
                energy = cols_ref[:, 24 + c * 4 + b : 25 + c * 4 + b] - hole_ref[c : c + 1, cols]
                value = (acc[rows, cols] + other) / energy
                usable = my * 512 + b * 128 + iota((128, 128), 0) < sizes_ref[c]
                out_ref[c, half, cols] = jnp.where(usable, value, 0.0).astype(BF)

    slot_cp.wait()
    back_cp.wait()
    last = 6 * n
    for m in range(last + LAG + TAIL):
        if m < last:
            if m % 6 == 0:
                fwd_wait(m // 6)
            produce(m)
        if 0 <= m - LAG < last:
            relay(m - LAG)
            if m - LAG == last - 1:
                for i in range(4):
                    send_on(0, i)
        d = m - LAG - TAIL
        if 0 <= d < last:
            total(d)
            k, q = divmod(d, 6)
            if k > 0 and q < 2:
                give_back(k - 1, 2 * q)
                give_back(k - 1, 2 * q + 1)
            if d == 11:
                arrive(0, 0)
            if 11 <= d < 15:
                collect(0, d - 11)
    give_quarter(2, 0)
    give_quarter(2, 1)
    final_relay(0)
    give_quarter(2, 2)
    give_quarter(2, 3)
    arrive(1, 0)
    for i in range(4):
        collect(1, i)
        send_on(1, i)
    for i in range(4):
        arrive(2, i)
        collect(2, i)
        send_on(2, i)
        if i == 0:
            final_relay(1)
    finish(0)
    finish(1)
    final_relay(2)
    finish(2)

    req_all.wait_send()
    for m in range(last):
        for i in range(6):
            cycle_rs(m, i).wait_send()
    for k in range(n):
        for i in range(6):
            final_rs(k, i).wait_send()


def per_device(
    block_sizes, amplitudes, ladder_coupling, bare_coupling, particle_energy, hole_energy,
    cycle_coupling, pandya_rows, pandya_weight,
):
    vmem = pl.BlockSpec(memory_space=pltpu.VMEM)
    smem = pl.BlockSpec(memory_space=pltpu.SMEM)
    hbm = pl.BlockSpec(memory_space=pl.ANY)
    n = CHUNKS
    scratch = [
        pltpu.SMEM((8, 512), I32),
        pltpu.SMEM((128, 128), I32),
        pltpu.VMEM((8, 512), I32),
        pltpu.VMEM((128, 128), I32),
        pltpu.VMEM((128, 128), F32),
        pltpu.VMEM((32, 4, 128), I32),
        pltpu.VMEM(amplitudes.shape, BF),
        pltpu.VMEM(bare_coupling.shape, BF),
        pltpu.VMEM((3, 2048, 512), BF),
        pltpu.VMEM((32, 4, 128), I32),
        pltpu.VMEM((4, 32, 128), I32),
        pltpu.VMEM((16 * CAP, 128), BF),
        pltpu.VMEM((4, 32 * CAP), I32),
        pltpu.VMEM((4, 32 * CAP, 128), I32),
        pltpu.VMEM((8 * CAP, 1024), BF),
        pltpu.VMEM((128 * CAP, 128), F32),
        pltpu.VMEM((2, 3072, 128), F32),
        pltpu.VMEM((512, 128), F32),
        pltpu.VMEM((512, 128), BF),
        pltpu.VMEM((CAP, 128), F32),
        pltpu.VMEM((1024, 384), F32),
    ]
    for shape in (
        (32, 4 * CAP, 128), (32, 4 * CAP, 128), (32, 4 * CAP, 128), (6, 2048, 128),
        (6, 2, 256, 128), (6, 2, 256, 128), (6, 2, 256, 128),
        (4096, 128), (2, 512, 128), (2, 512, 128), (2, 512, 128),
    ):
        scratch += [pltpu.VMEM(shape, BF)] * n
    sem = pltpu.SemaphoreType.DMA
    scratch += [
        sem((12,)), sem((3,)), sem, sem, sem((n,)), sem((n,)), sem((n, 6, 6)), sem((n, 6, 6)),
        sem((n,)), sem((n, 4)), sem((n, 6)), sem((n, 6)),
    ]
    return pl.pallas_call(
        main_kernel,
        out_shape=jax.ShapeDtypeStruct(bare_coupling.shape, BF),
        in_specs=[smem] + [vmem] * 4 + [hbm] * 4,
        out_specs=vmem,
        scratch_shapes=scratch,
        compiler_params=pltpu.CompilerParams(
            collective_id=0, has_side_effects=True, vmem_limit_bytes=60 * 1024 * 1024
        ),
        cost_estimate=pl.CostEstimate(flops=20_000_000_000, bytes_accessed=40_000_000, transcendentals=0),
    )(
        block_sizes, pandya_rows, pandya_weight, particle_energy, hole_energy,
        amplitudes, ladder_coupling, bare_coupling, cycle_coupling,
    )


def solution(mesh):
    in_specs = (
        P("chan"),
        P("chan", None, None),
        P("chan", "rep", None),
        P("chan", "rep", None),
        P("chan", "rep"),
        P("chan", None),
        P("chan", None, "rep"),
        P("chan", "rep"),
        P("chan", "rep"),
    )
    out_specs = P("chan", "rep", None)
    return jax.shard_map(
        per_device, mesh=mesh, in_specs=in_specs, out_specs=out_specs, check_vma=False
    )
```
